32 devices in a mesh: island: 2 (over core), fsdp: 4 (over z), tensor: 4 (over y, x).
Axes of the slice: x: 2, y: 2, z: 4, core: 2. Of those that a mesh axis runs over, the one named last changes fastest.
Arguments:
- tokens: bfloat16 [2048, 4608], P(('island', 'fsdp')), may hold values from -6 to 6
- cotangent: bfloat16 [2048, 4608], P(('island', 'fsdp')), may hold values from -0.19921875 to 0.19921875
- gate_tiles: bfloat16 [16, 4, 128, 128], P('fsdp', 'tensor'), may hold values from -1 to 1
- up_tiles: bfloat16 [16, 4, 128, 128], P('fsdp', 'tensor'), may hold values from -1 to 1
- gate_where: int32 [16, 4], P('fsdp', 'tensor'), may hold values from 0 to 2591, as said below
- up_where: int32 [16, 4], P('fsdp', 'tensor'), may hold values from 0 to 2591, as said below
- down_where: int32 [16, 4], P(None, 'tensor'), may hold values from 0 to 2591, as said below
- down_global: float32 [16, 4, 128, 128], P('fsdp', 'tensor'), may hold values from -6 to 6
- down_moment: float32 [16, 4, 128, 128], P('fsdp', 'tensor'), may hold values from -3 to 3
Outputs:
- new_global: float32 [16, 4, 128, 128], P('fsdp', 'tensor')
- new_moment: float32 [16, 4, 128, 128], P('fsdp', 'tensor')
The draws below stay inside these ranges and needn't reach their ends.
Inputs may be any that keep to these rules, and one draw needn't show every extreme that they name: In each column t, the 16 entries of gate_where are distinct cells r * 72 + c of the 36 x 72 tile grid of shard t (r a block of the model width, c a block of the shard's hidden units). In each column t, the 16 entries of up_where are distinct cells r * 72 + c of the 36 x 72 tile grid of shard t. In each column t, the 16 entries of down_where are distinct cells a * 36 + b, a a block of shard t's hidden units (72 of them) and b a block of the model width.
All inputs are finite; a program needn't handle non-finite values.
Results may differ from the reference program's by a relative error of at most 0.00057.
Values may be sent and summed in bfloat16 or wider, within the bound.
A program may use at most 128 MiB of HBM per device.

```python
import jax
import jax.numpy as jnp
from jax import lax

D = 4608
TILE = 128
DROWS = 36
FCOLS = 72
SHARDS = 4
KEPT = 16
ISLANDS = 2
ITOK = 1024
TOKENS = 2048


def pick_cells(key, cells):
    keys = jax.random.split(key, SHARDS + 3)

    def one_column(column_key):
        return jax.random.permutation(column_key, cells)[:KEPT]
    chosen = jax.vmap(one_column)(keys[:SHARDS])
    inner = 1 + jax.random.permutation(keys[SHARDS], cells - 2)[:KEPT - 2]
    ends = jnp.array([0, cells - 1], dtype=jnp.int32)
    special = jax.random.permutation(keys[SHARDS + 1], jnp.concatenate([ends, inner.astype(jnp.int32)]))
    column_at = jax.random.randint(keys[SHARDS + 2], (), 0, SHARDS)
    is_special = (jnp.arange(SHARDS, dtype=jnp.int32) == column_at)[:, None]
    chosen = jnp.where(is_special, special[None, :], chosen.astype(jnp.int32))
    return jnp.transpose(chosen).astype(jnp.int32)


def draw_gate_where(key, part):
    key = jax.random.fold_in(key, 11)
    return pick_cells(key, DROWS * FCOLS)


def draw_up_where(key, part):
    key = jax.random.fold_in(key, 12)
    return pick_cells(key, DROWS * FCOLS)


def draw_down_where(key, part):
    key = jax.random.fold_in(key, 13)
    return pick_cells(key, DROWS * FCOLS)


def levels(own_key, shape, cuts, low, top_value):
    def one(dim, shards_of):
        heights = jax.random.uniform(jax.random.fold_in(jax.random.fold_in(own_key, 6), dim), (shards_of,), jnp.float32, low / len(cuts), top_value / len(cuts))
        return jnp.repeat(jnp.exp(heights), shape[dim] // shards_of).reshape((-1,) + (1,) * (len(shape) - dim - 1))

    gain = one(*cuts[0])
    for cut in cuts[1:]:
        gain = gain * one(*cut)
    return gain


def noise(rng, dims, spread, bound, shards=(), held_as=jnp.bfloat16):
    values = spread * jax.random.normal(rng, dims, jnp.float32)
    if shards:
        values = values * levels(rng, dims, shards, -0.22, 0.18)
    return jnp.clip(values, -bound, bound).astype(held_as)


def setup_inputs(seed: int = 0) -> dict:
    streams_of = jax.random.split(jax.random.key(seed), 10)
    tokens = noise(streams_of[0], (TOKENS, D), 1.0, 6.0, ((0, 8),))
    cotangent = noise(streams_of[1], (TOKENS, D), 0.03125, 0.19921875, ((0, 8),))
    gate_tiles = noise(streams_of[2], (KEPT, SHARDS, TILE, TILE), (TILE * KEPT // FCOLS) ** -0.5, 1.0, ((0, 4), (1, 4)))
    up_tiles = noise(streams_of[3], (KEPT, SHARDS, TILE, TILE), (TILE * KEPT // FCOLS) ** -0.5, 1.0, ((0, 4), (1, 4)))
    gate_where = draw_gate_where(jax.random.fold_in(streams_of[9], 71), 0)
    up_where = draw_up_where(jax.random.fold_in(streams_of[9], 71), 0)
    down_where = draw_down_where(jax.random.fold_in(streams_of[9], 71), 0)
    down_global = noise(streams_of[7], (KEPT, SHARDS, TILE, TILE), 1.0, 6.0, ((0, 4), (1, 4)), jnp.float32)
    down_moment = noise(streams_of[8], (KEPT, SHARDS, TILE, TILE), 0.5, 3.0, ((0, 4), (1, 4)), jnp.float32)
    return {"tokens": tokens, "cotangent": cotangent, "gate_tiles": gate_tiles, "up_tiles": up_tiles, "gate_where": gate_where, "up_where": up_where, "down_where": down_where, "down_global": down_global, "down_moment": down_moment}


inner_rate = 0.5
decay_rate = 0.1
outer_rate = 0.7
momentum_rate = 0.9


def tile_project(tok_blocks, tiles, where, col_blocks):
    row_ids = where // col_blocks
    col_ids = where % col_blocks
    picked = jnp.take(tok_blocks, row_ids, axis=1).astype(jnp.float32)
    partial_value = jnp.einsum('tkr,krc->tkc', picked, tiles.astype(jnp.float32))
    onehot = (col_ids[:, None] == jnp.arange(col_blocks, dtype=jnp.int32)[None, :]).astype(jnp.float32)
    return jnp.einsum('tkc,kj->tjc', partial_value, onehot, precision=lax.Precision.HIGHEST)


def reference(tokens, cotangent, gate_tiles, up_tiles, gate_where, up_where, down_where, down_global, down_moment):
    tok_blocks = tokens.reshape(ISLANDS, ITOK, DROWS, TILE)
    cot_blocks = cotangent.reshape(ISLANDS, ITOK, DROWS, TILE)

    def one_shard(inputs):
        gate_part, up_part, gate_at, up_at, down_at, master, moment = inputs
        island_total = jnp.zeros((KEPT, TILE, TILE), jnp.float32)
        for island in range(ISLANDS):
            gate_sum = tile_project(tok_blocks[island], gate_part, gate_at, FCOLS)
            up_sum = tile_project(tok_blocks[island], up_part, up_at, FCOLS)
            hidden = (jax.nn.silu(gate_sum) * up_sum).astype(jnp.bfloat16)
            hidden_pick = jnp.take(hidden, down_at // DROWS, axis=1).astype(jnp.float32)
            cot_pick = jnp.take(cot_blocks[island], down_at % DROWS, axis=1).astype(jnp.float32)
            grad_tiles = jnp.einsum('tka,tkb->kab', hidden_pick, cot_pick)
            island_total = island_total + inner_rate * (grad_tiles + decay_rate * master)
        average = island_total / ISLANDS
        fresh_moment = momentum_rate * moment + average
        fresh_master = master - outer_rate * (average + momentum_rate * fresh_moment)
        return fresh_master, fresh_moment

    inputs = tuple(jnp.moveaxis(array, 1, 0) for array in (gate_tiles, up_tiles, gate_where, up_where, down_where, down_global, down_moment))
    fresh_master, fresh_moment = lax.map(one_shard, inputs)
    return jnp.moveaxis(fresh_master, 0, 1), jnp.moveaxis(fresh_moment, 0, 1)
```

```python
import functools

import jax
import jax.numpy as jnp
from jax import lax
from jax.experimental import pallas as pl
from jax.experimental.pallas import tpu as pltpu
from jax.sharding import PartitionSpec as P

FF = 36864
MESH = pl.DeviceIdType.MESH

inner_rate = 0.5
decay_rate = 0.1
outer_rate = 0.7
momentum_rate = 0.9


def steps(count, step):
    if count <= 4:
        for i in range(count):
            step(i)
    else:
        lax.fori_loop(0, count, lambda i, c: (step(i), c)[1], 0)


def arrival(i, z, n):
    close = jnp.minimum(z, n - 1 - z)
    near = jnp.where(i % 2 == 1, z - (i + 1) // 2, z + i // 2)
    far = jnp.where(z < n - 1 - z, i, n - 1 - i)
    return jnp.where(i <= 2 * close, near, far)


def departure(s, z, n):
    close = jnp.minimum(z, n - 1 - z)
    own = 2 * close + 1
    at = s + jnp.where(s >= own, 1, 0)
    side = jnp.where(at % 2 == 0, n - 1 - at // 2, (at - 1) // 2)
    side = jnp.where(z < n - 1 - z, side, n - 1 - side)
    return jnp.where(s == n - 1, z, side)


def kernel(
    n, groups, col_blocks,
    gate_at, up_at, down_at, gate_hbm, up_hbm, tok_hbm, cot_hbm,
    out_ref,
    tok, cot, w, meta, sums, own, give, take, moved, final, cross,
    meta_s, cols, rows, prev, last,
    in_sem, meta_ss, meta_rs, meta_ls, ag_ss, ag_rs, sis_ss, sis_rs,
    give_ss, give_rs, rs_ss, rs_rs, fin_ss, fin_rs, x_ss, x_rs,
):
    z = lax.axis_index("fsdp")
    isl = lax.axis_index("island")
    core = lax.rem(isl, 2)
    group = lax.div(isl, 2)
    sister = isl + 1 - 2 * core
    each = gate_hbm.shape[0]
    half = each // 2
    kept = n * each
    side = gate_hbm.shape[-1]
    row_blocks = tok_hbm.shape[1] // side

    local = [
        pltpu.make_async_copy(gate_hbm, w.at[0, z], in_sem.at[0]),
        pltpu.make_async_copy(up_hbm, w.at[1, z], in_sem.at[1]),
        pltpu.make_async_copy(tok, tok, in_sem.at[2]),
        pltpu.make_async_copy(cot, cot, in_sem.at[3]),
    ]
    local[0].start()
    local[1].start()

    barrier = pltpu.get_barrier_semaphore()
    for off in range(1, n):
        pl.semaphore_signal(barrier, inc=1, device_id={"fsdp": lax.rem(z + off, n)}, device_id_type=MESH)
    pl.semaphore_signal(barrier, inc=1, device_id={"island": sister}, device_id_type=MESH)
    for off in range(1, groups):
        peer = lax.rem(group + off, groups) * 2 + core
        pl.semaphore_signal(barrier, inc=1, device_id={"island": peer}, device_id_type=MESH)

    for b in range(row_blocks):
        pltpu.make_async_copy(
            tok_hbm.at[:, pl.ds(b * side, side)], tok.at[b], in_sem.at[2]).start()
    for b in range(row_blocks):
        pltpu.make_async_copy(
            cot_hbm.at[:, pl.ds(b * side, side)], cot.at[b], in_sem.at[3]).start()

    row_i = lax.broadcasted_iota(jnp.int32, (2 * each, side), 0)
    lane_i = lax.broadcasted_iota(jnp.int32, (2 * each, side), 1)
    packed = jnp.zeros((2 * each, side), jnp.int32)
    for q in range(2 * each):
        cell = gate_at[q, 0] if q < each else up_at[q - each, 0]
        r = lax.div(cell, col_blocks)
        c = cell - r * col_blocks
        packed = jnp.where(row_i == q, jnp.where(lane_i == 0, r, c), packed)
    meta[z] = packed
    zero = jnp.zeros(sums.shape[2:], jnp.float32)
    sums[0, kept] = zero
    sums[1, kept] = zero

    pl.semaphore_wait(barrier, n + groups - 1)

    def meta_copy(off):
        return pltpu.make_async_remote_copy(
            src_ref=meta.at[z], dst_ref=meta.at[z],
            send_sem=meta_ss.at[off], recv_sem=meta_rs.at[z],
            device_id={"fsdp": lax.rem(z + off, n)}, device_id_type=MESH)

    def meta_arrived(p):
        return pltpu.make_async_remote_copy(
            src_ref=meta.at[p], dst_ref=meta.at[p],
            send_sem=meta_ss.at[0], recv_sem=meta_rs.at[p],
            device_id={"fsdp": p}, device_id_type=MESH)

    for off in range(1, n):
        meta_copy(off).start()
    local[0].wait()
    local[1].wait()

    def line(c, sub, up):
        to = jnp.minimum(z + 1, n - 1) if up else jnp.maximum(z - 1, 0)
        part = w.at[core, c, pl.ds(sub * half, half)]
        return pltpu.make_async_remote_copy(
            src_ref=part, dst_ref=part,
            send_sem=ag_ss.at[0 if up else 1, c, sub], recv_sem=ag_rs.at[c, sub],
            device_id={"fsdp": to}, device_id_type=MESH)

    def share(c, sub, which):
        part = w.at[which, c, pl.ds(sub * half, half)]
        return pltpu.make_async_remote_copy(
            src_ref=part, dst_ref=part,
            send_sem=sis_ss.at[c, sub], recv_sem=sis_rs.at[c, sub],
            device_id={"island": sister}, device_id_type=MESH)

    for sub in range(2):
        @pl.when(z < n - 1)
        def _():
            line(z, sub, True).start()

        @pl.when(z > 0)
        def _():
            line(z, sub, False).start()

    def forward(i):
        c = arrival(i, z, n)
        for sub in range(2):
            line(c, sub, True).wait_recv()

            @pl.when((c < z) & (z < n - 1))
            def _():
                line(c, sub, True).start()

            @pl.when((c > z) & (z > 0))
            def _():
                line(c, sub, False).start()

            share(c, sub, core).start()

    def tables():
        for off in range(1, n):
            meta_arrived(lax.rem(z + off, n)).wait_recv()
        copy = pltpu.make_async_copy(meta, meta_s, meta_ls)
        copy.start()
        copy.wait()
        for m in range(2):
            def read(i):
                c = arrival(i, z, n)
                for t in range(each):
                    rows[m, i * each + t] = meta_s[c, m * each + t, 0]
                    cols[m, i * each + t] = meta_s[c, m * each + t, 1]

            steps(n, read)

            def link(i, carry):
                mine = cols[m, i]
                wanted = lax.div(down_at[i, 0], row_blocks)
                before = jnp.int32(kept)
                found = jnp.int32(kept)
                for k in range(kept):
                    there = cols[m, k]
                    before = jnp.where((there == mine) & (k < i), k, before)
                    found = jnp.where(there == wanted, k, found)
                prev[m, i] = before
                last[m, i] = found
                return carry

            lax.fori_loop(0, kept, link, 0)

    def project(i):
        c = arrival(i, z, n)
        for t in range(each):
            slot = i * each + t
            for m in range(2):
                x = tok[rows[m, slot]]
                sums[m, slot] = sums[m, prev[m, slot]] + jnp.dot(
                    x, w[m, c, t], preferred_element_type=jnp.float32)

    def gather(i):
        if n <= 4:
            if i + 1 < n:
                forward(i + 1)
        else:
            @pl.when(i + 1 < n)
            def _():
                forward(i + 1)

        if n <= 4:
            if i == 0:
                tables()
                local[2].wait()
            else:
                c = arrival(i, z, n)
                for sub in range(2):
                    share(c, sub, 1 - core).wait_recv()
        else:
            @pl.when(i == 0)
            def _():
                tables()
                local[2].wait()

            @pl.when(i > 0)
            def _():
                c = arrival(i, z, n)
                for sub in range(2):
                    share(c, sub, 1 - core).wait_recv()
        project(i)

    steps(n, gather)
    local[3].wait()

    def pair(d, u):
        return pltpu.make_async_remote_copy(
            src_ref=give.at[d, u], dst_ref=take.at[d, u],
            send_sem=give_ss.at[d, u], recv_sem=give_rs.at[d, u],
            device_id={"island": sister}, device_id_type=MESH)

    def grad(j):
        g = sums[0, last[0, j]]
        u = sums[1, last[1, j]]
        e = jnp.exp(-jnp.abs(g))
        hidden = (g * jnp.where(g >= 0, 1.0, e) / (1.0 + e) * u).astype(jnp.bfloat16)
        return lax.dot_general(
            hidden, cot[lax.rem(down_at[j, 0], row_blocks)], (((0,), (0,)), ((), ())),
            preferred_element_type=jnp.float32)

    def make(s):
        d = departure(s, z, n)
        for u in range(half):
            give[d, u] = grad(d * each + (1 - core) * half + u)
            pair(d, u).start()
        for u in range(half):
            own[d, u] = grad(d * each + core * half + u)

    def hop(d, u):
        up = jnp.where(d > z, 0, 1)
        to = jnp.where(d > z, jnp.minimum(z + 1, n - 1), jnp.maximum(z - 1, 0))
        return pltpu.make_async_remote_copy(
            src_ref=own.at[d, u], dst_ref=moved.at[up, d, u],
            send_sem=rs_ss.at[d, u], recv_sem=rs_rs.at[up, d, u],
            device_id={"fsdp": to}, device_id_type=MESH)

    def came(up, d, u):
        return pltpu.make_async_remote_copy(
            src_ref=own.at[d, u], dst_ref=moved.at[up, d, u],
            send_sem=rs_ss.at[d, u], recv_sem=rs_rs.at[up, d, u],
            device_id={"fsdp": z}, device_id_type=MESH)

    def pass_on(s):
        d = departure(s, z, n)
        up = jnp.where(d > z, 0, 1)
        middle = (z > 0) & (z < n - 1)
        for u in range(half):
            pair(d, u).wait_recv()

            @pl.when(middle)
            def _():
                came(up, d, u).wait_recv()
                own[d, u] = own[d, u] + take[d, u] + moved[up, d, u]

            @pl.when(jnp.logical_not(middle))
            def _():
                own[d, u] = own[d, u] + take[d, u]

            hop(d, u).start()

    make(0)

    def scatter(s):
        make(s + 1)
        pass_on(s)

    steps(n - 1, scatter)

    def last_hop(u):
        part = final.at[core * half + u]
        return pltpu.make_async_remote_copy(
            src_ref=part, dst_ref=part, send_sem=fin_ss.at[u], recv_sem=fin_rs.at[u],
            device_id={"island": sister}, device_id_type=MESH)

    def other_hop(u):
        part = final.at[(1 - core) * half + u]
        return pltpu.make_async_remote_copy(
            src_ref=part, dst_ref=part, send_sem=fin_ss.at[u], recv_sem=fin_rs.at[u],
            device_id={"island": sister}, device_id_type=MESH)

    def cross_hop(off, u):
        peer = lax.rem(group + off, groups) * 2 + core
        return pltpu.make_async_remote_copy(
            src_ref=cross.at[group, u], dst_ref=cross.at[group, u],
            send_sem=x_ss.at[off, u], recv_sem=x_rs.at[group, u],
            device_id={"island": peer}, device_id_type=MESH)

    def cross_came(off, u):
        there = lax.rem(group + off, groups)
        return pltpu.make_async_remote_copy(
            src_ref=cross.at[there, u], dst_ref=cross.at[there, u],
            send_sem=x_ss.at[off, u], recv_sem=x_rs.at[there, u],
            device_id={"island": there * 2 + core}, device_id_type=MESH)

    for u in range(half):
        pair(z, u).wait_recv()
        own[z, u] = own[z, u] + take[z, u]

        @pl.when(z > 0)
        def _():
            came(0, z, u).wait_recv()
            own[z, u] = own[z, u] + moved[0, z, u]

        @pl.when(z < n - 1)
        def _():
            came(1, z, u).wait_recv()
            own[z, u] = own[z, u] + moved[1, z, u]

        if groups > 1:
            cross[group, u] = own[z, u]
            for off in range(1, groups):
                cross_hop(off, u).start()
            for off in range(1, groups):
                cross_came(off, u).wait_recv()
            total = cross[0, u]
            for g in range(1, groups):
                total = total + cross[g, u]
            final[core * half + u] = total
        else:
            final[core * half + u] = own[z, u]
        last_hop(u).start()

    for u in range(half):
        other_hop(u).wait_recv()
    out_ref[...] = final[...]

    for u in range(half):
        last_hop(u).wait_send()
        for off in range(1, groups):
            cross_hop(off, u).wait_send()
    for off in range(1, n):
        meta_copy(off).wait_send()

    def drain(c):
        for sub in range(2):
            @pl.when((c <= z) & (z < n - 1))
            def _():
                line(c, sub, True).wait_send()

            @pl.when((c >= z) & (z > 0))
            def _():
                line(c, sub, False).wait_send()

            @pl.when(c != z)
            def _():
                share(c, sub, core).wait_send()
        for u in range(half):
            pair(c, u).wait_send()

            @pl.when(c != z)
            def _():
                hop(c, u).wait_send()

    steps(n, drain)


def body(
    tokens,
    cotangent,
    gate_tiles,
    up_tiles,
    gate_where,
    up_where,
    down_where,
    down_global,
    down_moment,
):
    n = lax.axis_size("fsdp")
    islands = lax.axis_size("island")
    groups = islands // 2
    each, _, side, _ = gate_tiles.shape
    half = each // 2
    kept = n * each
    count, width = tokens.shape
    col_blocks = FF // side // lax.axis_size("tensor")
    f32, bf16, i32 = jnp.float32, jnp.bfloat16, jnp.int32
    dma = pltpu.SemaphoreType.DMA
    smem = pl.BlockSpec(memory_space=pltpu.SMEM)
    anyw = pl.BlockSpec(memory_space=pl.ANY)
    summed = pl.pallas_call(
        functools.partial(kernel, n, groups, col_blocks),
        out_shape=jax.ShapeDtypeStruct((each, side, side), f32),
        in_specs=[smem] * 3 + [anyw] * 4,
        out_specs=pl.BlockSpec(memory_space=pltpu.VMEM),
        scratch_shapes=[
            pltpu.VMEM((width // side, count, side), bf16),
            pltpu.VMEM((width // side, count, side), bf16),
            pltpu.VMEM((2, n, each, side, side), bf16),
            pltpu.VMEM((n, 2 * each, side), i32),
            pltpu.VMEM((2, kept + 1, count, side), f32),
            pltpu.VMEM((n, half, side, side), f32),
            pltpu.VMEM((n, half, side, side), f32),
            pltpu.VMEM((n, half, side, side), f32),
            pltpu.VMEM((2, n, half, side, side), f32),
            pltpu.VMEM((each, side, side), f32),
            pltpu.VMEM((groups, half, side, side), f32),
            pltpu.SMEM((n, 2 * each, side), i32),
            pltpu.SMEM((2, kept), i32),
            pltpu.SMEM((2, kept), i32),
            pltpu.SMEM((2, kept), i32),
            pltpu.SMEM((2, kept), i32),
            dma((4,)),
            dma((n,)),
            dma((n,)),
            dma,
            dma((2, n, 2)),
            dma((n, 2)),
            dma((n, 2)),
            dma((n, 2)),
            dma((n, half)),
            dma((n, half)),
            dma((n, half)),
            dma((2, n, half)),
            dma((half,)),
            dma((half,)),
            dma((groups, half)),
            dma((groups, half)),
        ],
        compiler_params=pltpu.CompilerParams(
            collective_id=0, has_side_effects=True, vmem_limit_bytes=60 * 1024 * 1024
        ),
        cost_estimate=pl.CostEstimate(
            flops=6 * kept * count * side * side,
            bytes_accessed=2 * tokens.size * 2,
            transcendentals=kept * count * side,
        ),
    )(gate_where, up_where, down_where, gate_tiles[:, 0], up_tiles[:, 0], tokens, cotangent)
    master = down_global[:, 0]
    moment = down_moment[:, 0]
    average = inner_rate * (summed / islands + decay_rate * master)
    fresh_moment = momentum_rate * moment + average
    fresh_master = master - outer_rate * (average + momentum_rate * fresh_moment)
    return (fresh_master[:, None], fresh_moment[:, None])


def solution(mesh):
    placed = (
        P(("island", "fsdp"), None),
        P(("island", "fsdp"), None),
        P("fsdp", "tensor", None, None),
        P("fsdp", "tensor", None, None),
        P("fsdp", "tensor"),
        P("fsdp", "tensor"),
        P(None, "tensor"),
        P("fsdp", "tensor", None, None),
        P("fsdp", "tensor", None, None),
    )
    return jax.shard_map(
        body,
        mesh=mesh,
        in_specs=placed,
        out_specs=(P("fsdp", "tensor", None, None), P("fsdp", "tensor", None, None)),
        check_vma=False,
    )
```

```python
import functools

import jax
import jax.numpy as jnp
from jax import lax
from jax.experimental import pallas as pl
from jax.experimental.pallas import tpu as pltpu
from jax.sharding import PartitionSpec as P

FF = 36864
MESH = pl.DeviceIdType.MESH

inner_rate = 0.5
decay_rate = 0.1
outer_rate = 0.7
momentum_rate = 0.9


def steps(count, step):
    if count <= 4:
        for i in range(count):
            step(i)
    else:
        lax.fori_loop(0, count, lambda i, c: (step(i), c)[1], 0)


def arrival(i, z, n):
    close = jnp.minimum(z, n - 1 - z)
    near = jnp.where(i % 2 == 1, z - (i + 1) // 2, z + i // 2)
    far = jnp.where(z < n - 1 - z, i, n - 1 - i)
    return jnp.where(i <= 2 * close, near, far)


def departure(s, z, n):
    close = jnp.minimum(z, n - 1 - z)
    own = 2 * close + 1
    at = s + jnp.where(s >= own, 1, 0)
    side = jnp.where(at % 2 == 0, n - 1 - at // 2, (at - 1) // 2)
    side = jnp.where(z < n - 1 - z, side, n - 1 - side)
    return jnp.where(s == n - 1, z, side)


def kernel(
    n, groups, col_blocks,
    gate_at, up_at, down_at, gate_hbm, up_hbm, tok_hbm, cot_hbm,
    out_ref,
    tok, cot, w, meta, sums, prod, own, give, take, moved, final, cross,
    meta_s, cols, rows, prev, last,
    in_sem, meta_ss, meta_rs, meta_ls, ag_ss, ag_rs, sis_ss, sis_rs,
    give_ss, give_rs, rs_ss, rs_rs, fin_ss, fin_rs, x_ss, x_rs,
):
    z = lax.axis_index("fsdp")
    isl = lax.axis_index("island")
    core = lax.rem(isl, 2)
    group = lax.div(isl, 2)
    sister = isl + 1 - 2 * core
    each = gate_hbm.shape[0]
    half = each // 2
    kept = n * each
    side = gate_hbm.shape[-1]
    row_blocks = tok_hbm.shape[1] // side

    local = [
        pltpu.make_async_copy(gate_hbm, w.at[0, z], in_sem.at[0]),
        pltpu.make_async_copy(up_hbm, w.at[1, z], in_sem.at[1]),
        pltpu.make_async_copy(tok, tok, in_sem.at[2]),
        pltpu.make_async_copy(cot, cot, in_sem.at[3]),
    ]
    local[0].start()
    local[1].start()

    barrier = pltpu.get_barrier_semaphore()
    for off in range(1, n):
        pl.semaphore_signal(barrier, inc=1, device_id={"fsdp": lax.rem(z + off, n)}, device_id_type=MESH)
    pl.semaphore_signal(barrier, inc=1, device_id={"island": sister}, device_id_type=MESH)
    for off in range(1, groups):
        peer = lax.rem(group + off, groups) * 2 + core
        pl.semaphore_signal(barrier, inc=1, device_id={"island": peer}, device_id_type=MESH)

    row_i = lax.broadcasted_iota(jnp.int32, (2 * each, side), 0)
    lane_i = lax.broadcasted_iota(jnp.int32, (2 * each, side), 1)
    packed = jnp.zeros((2 * each, side), jnp.int32)
    for q in range(2 * each):
        cell = gate_at[0, q] if q < each else up_at[0, q - each]
        r = lax.div(cell, col_blocks)
        c = cell - r * col_blocks
        packed = jnp.where(row_i == q, jnp.where(lane_i == 0, r, c), packed)
    meta[z] = packed
    zero = jnp.zeros(sums.shape[2:], jnp.float32)
    sums[0, kept] = zero
    sums[1, kept] = zero

    pl.semaphore_wait(barrier, n + groups - 1)

    def meta_copy(off):
        return pltpu.make_async_remote_copy(
            src_ref=meta.at[z], dst_ref=meta.at[z],
            send_sem=meta_ss.at[off], recv_sem=meta_rs.at[z],
            device_id={"fsdp": lax.rem(z + off, n)}, device_id_type=MESH)

    def meta_arrived(p):
        return pltpu.make_async_remote_copy(
            src_ref=meta.at[p], dst_ref=meta.at[p],
            send_sem=meta_ss.at[0], recv_sem=meta_rs.at[p],
            device_id={"fsdp": p}, device_id_type=MESH)

    for off in range(1, n):
        meta_copy(off).start()
    local[0].wait()
    local[1].wait()

    def line(c, sub, up):
        to = jnp.minimum(z + 1, n - 1) if up else jnp.maximum(z - 1, 0)
        part = w.at[core, c, pl.ds(sub * half, half)]
        return pltpu.make_async_remote_copy(
            src_ref=part, dst_ref=part,
            send_sem=ag_ss.at[0 if up else 1, c, sub], recv_sem=ag_rs.at[c, sub],
            device_id={"fsdp": to}, device_id_type=MESH)

    def share(c, sub, which):
        part = w.at[which, c, pl.ds(sub * half, half)]
        return pltpu.make_async_remote_copy(
            src_ref=part, dst_ref=part,
            send_sem=sis_ss.at[c, sub], recv_sem=sis_rs.at[c, sub],
            device_id={"island": sister}, device_id_type=MESH)

    for sub in range(2):
        @pl.when(z < n - 1)
        def _():
            line(z, sub, True).start()

        @pl.when(z > 0)
        def _():
            line(z, sub, False).start()

    for b in range(row_blocks):
        pltpu.make_async_copy(
            tok_hbm.at[:, pl.ds(b * side, side)], tok.at[b], in_sem.at[2]).start()
    for b in range(row_blocks):
        pltpu.make_async_copy(
            cot_hbm.at[:, pl.ds(b * side, side)], cot.at[b], in_sem.at[3]).start()

    def forward(i):
        c = arrival(i, z, n)
        for sub in range(2):
            line(c, sub, True).wait_recv()

            @pl.when((c < z) & (z < n - 1))
            def _():
                line(c, sub, True).start()

            @pl.when((c > z) & (z > 0))
            def _():
                line(c, sub, False).start()

            share(c, sub, core).start()

    def tables():
        for off in range(1, n):
            meta_arrived(lax.rem(z + off, n)).wait_recv()
        copy = pltpu.make_async_copy(meta, meta_s, meta_ls)
        copy.start()
        copy.wait()
        for m in range(2):
            def read(i):
                c = arrival(i, z, n)
                for t in range(each):
                    rows[m, i * each + t] = meta_s[c, m * each + t, 0]
                    cols[m, i * each + t] = meta_s[c, m * each + t, 1]

            steps(n, read)

            def link(i, carry):
                mine = cols[m, i]
                wanted = lax.div(down_at[0, i], row_blocks)
                before = jnp.int32(kept)
                found = jnp.int32(kept)
                for k in range(kept):
                    there = cols[m, k]
                    before = jnp.where((there == mine) & (k < i), k, before)
                    found = jnp.where(there == wanted, k, found)
                prev[m, i] = before
                last[m, i] = found
                return carry

            lax.fori_loop(0, kept, link, 0)

    def project(i):
        c = arrival(i, z, n)
        for m in range(2):
            for t in range(each):
                prod[m, t] = jnp.dot(
                    tok[rows[m, i * each + t]], w[m, c, t], preferred_element_type=jnp.float32)
        for t in range(each):
            slot = i * each + t
            for m in range(2):
                sums[m, slot] = sums[m, prev[m, slot]] + prod[m, t]

    def shared(i):
        c = arrival(i, z, n)
        for sub in range(2):
            share(c, sub, 1 - core).wait_recv()

    def start():
        tables()
        local[2].wait()
        project(0)

    middle = (z > 0) & (z < n - 1)
    if n == 4:
        @pl.when(middle)
        def _():
            for i in range(1, n - 1):
                forward(i)
            tables()
            local[2].wait()
            forward(n - 1)
            project(0)
            for i in range(1, n):
                shared(i)
                project(i)

        @pl.when(jnp.logical_not(middle))
        def _():
            start()
            for i in range(1, n):
                forward(i)
                if 1 < i < n - 1:
                    shared(i - 1)
                    project(i - 1)
                if 1 < i == n - 2:
                    shared(i)
                    project(i)
            shared(n - 1)
            project(n - 1)
    else:
        forward(1)
        start()

        def gather(i, carry):
            @pl.when(i + 1 < n)
            def _():
                forward(i + 1)

            shared(i)
            project(i)
            return carry

        lax.fori_loop(1, n, gather, 0)
    local[3].wait()

    def pair(d, u):
        return pltpu.make_async_remote_copy(
            src_ref=give.at[d, u], dst_ref=take.at[d, u],
            send_sem=give_ss.at[d, u], recv_sem=give_rs.at[d, u],
            device_id={"island": sister}, device_id_type=MESH)

    def grad(j):
        g = sums[0, last[0, j]]
        u = sums[1, last[1, j]]
        e = jnp.exp(-jnp.abs(g))
        hidden = (g * jnp.where(g >= 0, 1.0, e) / (1.0 + e) * u).astype(jnp.bfloat16)
        return lax.dot_general(
            hidden, cot[lax.rem(down_at[0, j], row_blocks)], (((0,), (0,)), ((), ())),
            preferred_element_type=jnp.float32)

    def make(s):
        d = departure(s, z, n)
        for u in range(half):
            give[d, u] = grad(d * each + (1 - core) * half + u)
        for u in range(half):
            pair(d, u).start()
        for u in range(half):
            own[d, u] = grad(d * each + core * half + u)

    def hop(d, u):
        up = jnp.where(d > z, 0, 1)
        to = jnp.where(d > z, jnp.minimum(z + 1, n - 1), jnp.maximum(z - 1, 0))
        return pltpu.make_async_remote_copy(
            src_ref=own.at[d, u], dst_ref=moved.at[up, d, u],
            send_sem=rs_ss.at[d, u], recv_sem=rs_rs.at[up, d, u],
            device_id={"fsdp": to}, device_id_type=MESH)

    def came(up, d, u):
        return pltpu.make_async_remote_copy(
            src_ref=own.at[d, u], dst_ref=moved.at[up, d, u],
            send_sem=rs_ss.at[d, u], recv_sem=rs_rs.at[up, d, u],
            device_id={"fsdp": z}, device_id_type=MESH)

    def pass_on(s):
        d = departure(s, z, n)
        up = jnp.where(d > z, 0, 1)
        for u in range(half):
            pair(d, u).wait_recv()

            @pl.when(middle)
            def _():
                came(up, d, u).wait_recv()
                own[d, u] = own[d, u] + take[d, u] + moved[up, d, u]

            @pl.when(jnp.logical_not(middle))
            def _():
                own[d, u] = own[d, u] + take[d, u]

            hop(d, u).start()

    def scatter(s):
        make(s + 1)
        pass_on(s)

    if n == 4:
        @pl.when(middle)
        def _():
            for s in range(n):
                make(s)
            for s in range(n - 1):
                pass_on(s)

        @pl.when(jnp.logical_not(middle))
        def _():
            make(0)
            for s in range(n - 1):
                scatter(s)
    else:
        make(0)
        steps(n - 1, scatter)

    def last_hop(u):
        part = final.at[core * half + u]
        return pltpu.make_async_remote_copy(
            src_ref=part, dst_ref=part, send_sem=fin_ss.at[u], recv_sem=fin_rs.at[u],
            device_id={"island": sister}, device_id_type=MESH)

    def other_hop(u):
        part = final.at[(1 - core) * half + u]
        return pltpu.make_async_remote_copy(
            src_ref=part, dst_ref=part, send_sem=fin_ss.at[u], recv_sem=fin_rs.at[u],
            device_id={"island": sister}, device_id_type=MESH)

    def cross_hop(off, u):
        peer = lax.rem(group + off, groups) * 2 + core
        return pltpu.make_async_remote_copy(
            src_ref=cross.at[group, u], dst_ref=cross.at[group, u],
            send_sem=x_ss.at[off, u], recv_sem=x_rs.at[group, u],
            device_id={"island": peer}, device_id_type=MESH)

    def cross_came(off, u):
        there = lax.rem(group + off, groups)
        return pltpu.make_async_remote_copy(
            src_ref=cross.at[there, u], dst_ref=cross.at[there, u],
            send_sem=x_ss.at[off, u], recv_sem=x_rs.at[there, u],
            device_id={"island": there * 2 + core}, device_id_type=MESH)

    for u in range(half):
        pair(z, u).wait_recv()
        own[z, u] = own[z, u] + take[z, u]

        @pl.when(z > 0)
        def _():
            came(0, z, u).wait_recv()
            own[z, u] = own[z, u] + moved[0, z, u]

        @pl.when(z < n - 1)
        def _():
            came(1, z, u).wait_recv()
            own[z, u] = own[z, u] + moved[1, z, u]

        if groups > 1:
            cross[group, u] = own[z, u]
            for off in range(1, groups):
                cross_hop(off, u).start()
            for off in range(1, groups):
                cross_came(off, u).wait_recv()
            total = cross[0, u]
            for g in range(1, groups):
                total = total + cross[g, u]
            final[core * half + u] = total
        else:
            final[core * half + u] = own[z, u]
        last_hop(u).start()

    for u in range(half):
        other_hop(u).wait_recv()
    out_ref[...] = final[...]

    for u in range(half):
        last_hop(u).wait_send()
        for off in range(1, groups):
            cross_hop(off, u).wait_send()
    for off in range(1, n):
        meta_copy(off).wait_send()

    def drain(c):
        for sub in range(2):
            @pl.when((c <= z) & (z < n - 1))
            def _():
                line(c, sub, True).wait_send()

            @pl.when((c >= z) & (z > 0))
            def _():
                line(c, sub, False).wait_send()

            @pl.when(c != z)
            def _():
                share(c, sub, core).wait_send()
        for u in range(half):
            pair(c, u).wait_send()

            @pl.when(c != z)
            def _():
                hop(c, u).wait_send()

    steps(n, drain)


def body(
    tokens,
    cotangent,
    gate_tiles,
    up_tiles,
    gate_where,
    up_where,
    down_where,
    down_global,
    down_moment,
):
    n = lax.axis_size("fsdp")
    islands = lax.axis_size("island")
    groups = islands // 2
    each, _, side, _ = gate_tiles.shape
    half = each // 2
    kept = n * each
    count, width = tokens.shape
    col_blocks = FF // side // lax.axis_size("tensor")
    f32, bf16, i32 = jnp.float32, jnp.bfloat16, jnp.int32
    dma = pltpu.SemaphoreType.DMA
    smem = pl.BlockSpec(memory_space=pltpu.SMEM)
    anyw = pl.BlockSpec(memory_space=pl.ANY)
    summed = pl.pallas_call(
        functools.partial(kernel, n, groups, col_blocks),
        out_shape=jax.ShapeDtypeStruct((each, side, side), f32),
        in_specs=[smem] * 3 + [anyw] * 4,
        out_specs=pl.BlockSpec(memory_space=pltpu.VMEM),
        scratch_shapes=[
            pltpu.VMEM((width // side, count, side), bf16),
            pltpu.VMEM((width // side, count, side), bf16),
            pltpu.VMEM((2, n, each, side, side), bf16),
            pltpu.VMEM((n, 2 * each, side), i32),
            pltpu.VMEM((2, kept + 1, count, side), f32),
            pltpu.VMEM((2, each, count, side), f32),
            pltpu.VMEM((n, half, side, side), f32),
            pltpu.VMEM((n, half, side, side), f32),
            pltpu.VMEM((n, half, side, side), f32),
            pltpu.VMEM((2, n, half, side, side), f32),
            pltpu.VMEM((each, side, side), f32),
            pltpu.VMEM((groups, half, side, side), f32),
            pltpu.SMEM((n, 2 * each, side), i32),
            pltpu.SMEM((2, kept), i32),
            pltpu.SMEM((2, kept), i32),
            pltpu.SMEM((2, kept), i32),
            pltpu.SMEM((2, kept), i32),
            dma((4,)),
            dma((n,)),
            dma((n,)),
            dma,
            dma((2, n, 2)),
            dma((n, 2)),
            dma((n, 2)),
            dma((n, 2)),
            dma((n, half)),
            dma((n, half)),
            dma((n, half)),
            dma((2, n, half)),
            dma((half,)),
            dma((half,)),
            dma((groups, half)),
            dma((groups, half)),
        ],
        compiler_params=pltpu.CompilerParams(
            collective_id=0, has_side_effects=True, vmem_limit_bytes=60 * 1024 * 1024
        ),
        cost_estimate=pl.CostEstimate(
            flops=6 * kept * count * side * side,
            bytes_accessed=2 * tokens.size * 2,
            transcendentals=kept * count * side,
        ),
    )(gate_where.T, up_where.T, down_where.T, gate_tiles[:, 0], up_tiles[:, 0], tokens, cotangent)
    master = down_global[:, 0]
    moment = down_moment[:, 0]
    average = inner_rate * (summed / islands + decay_rate * master)
    fresh_moment = momentum_rate * moment + average
    fresh_master = master - outer_rate * (average + momentum_rate * fresh_moment)
    return (fresh_master[:, None], fresh_moment[:, None])


def solution(mesh):
    placed = (
        P(("island", "fsdp"), None),
        P(("island", "fsdp"), None),
        P("fsdp", "tensor", None, None),
        P("fsdp", "tensor", None, None),
        P("fsdp", "tensor"),
        P("fsdp", "tensor"),
        P(None, "tensor"),
        P("fsdp", "tensor", None, None),
        P("fsdp", "tensor", None, None),
    )
    return jax.shard_map(
        body,
        mesh=mesh,
        in_specs=placed,
        out_specs=(P("fsdp", "tensor", None, None), P("fsdp", "tensor", None, None)),
        check_vma=False,
    )
```

```python
import functools

import jax
import jax.numpy as jnp
from jax import lax
from jax.experimental import pallas as pl
from jax.experimental.pallas import tpu as pltpu
from jax.sharding import PartitionSpec as P

FF = 36864
MESH = pl.DeviceIdType.MESH

inner_rate = 0.5
decay_rate = 0.1
outer_rate = 0.7
momentum_rate = 0.9


def steps(count, step):
    if count <= 4:
        for i in range(count):
            step(i)
    else:
        lax.fori_loop(0, count, lambda i, c: (step(i), c)[1], 0)


def arrival(i, z, n):
    close = jnp.minimum(z, n - 1 - z)
    near = jnp.where(i % 2 == 1, z - (i + 1) // 2, z + i // 2)
    far = jnp.where(z < n - 1 - z, i, n - 1 - i)
    return jnp.where(i <= 2 * close, near, far)


def departure(s, z, n):
    close = jnp.minimum(z, n - 1 - z)
    own = 2 * close + 1
    at = s + jnp.where(s >= own, 1, 0)
    side = jnp.where(at % 2 == 0, n - 1 - at // 2, (at - 1) // 2)
    side = jnp.where(z < n - 1 - z, side, n - 1 - side)
    return jnp.where(s == n - 1, z, side)


def kernel(
    n, groups, col_blocks,
    gate_at, up_at, down_at, gate_hbm, up_hbm, tok_hbm, cot_hbm,
    out_ref,
    tok, cot, w, meta, sums, prod, own, give, take, moved, final, cross,
    wants, plan, plan_s,
    in_sem, meta_ss, meta_rs, meta_ls, ag_ss, ag_rs, sis_ss, sis_rs,
    give_ss, give_rs, rs_ss, rs_rs, fin_ss, fin_rs, x_ss, x_rs,
):
    z = lax.axis_index("fsdp")
    isl = lax.axis_index("island")
    core = lax.rem(isl, 2)
    group = lax.div(isl, 2)
    sister = isl + 1 - 2 * core
    each = gate_hbm.shape[0]
    half = each // 2
    kept = n * each
    side = gate_hbm.shape[-1]
    row_blocks = tok_hbm.shape[1] // side

    local = [
        pltpu.make_async_copy(gate_hbm, w.at[0, z], in_sem.at[0]),
        pltpu.make_async_copy(up_hbm, w.at[1, z], in_sem.at[1]),
        pltpu.make_async_copy(tok, tok, in_sem.at[2]),
        pltpu.make_async_copy(cot, cot, in_sem.at[3]),
    ]
    local[0].start()
    local[1].start()

    barrier = pltpu.get_barrier_semaphore()
    for off in range(1, n):
        pl.semaphore_signal(barrier, inc=1, device_id={"fsdp": lax.rem(z + off, n)}, device_id_type=MESH)
    pl.semaphore_signal(barrier, inc=1, device_id={"island": sister}, device_id_type=MESH)
    for off in range(1, groups):
        peer = lax.rem(group + off, groups) * 2 + core
        pl.semaphore_signal(barrier, inc=1, device_id={"island": peer}, device_id_type=MESH)

    row_i = lax.broadcasted_iota(jnp.int32, (4 * each, side), 0)
    packed = jnp.zeros((4 * each, side), jnp.int32)
    for q in range(2 * each):
        cell = gate_at[0, q] if q < each else up_at[0, q - each]
        r = lax.div(cell, col_blocks)
        c = cell - r * col_blocks
        packed = jnp.where(row_i == q, c, jnp.where(row_i == 2 * each + q, r, packed))
    meta[z] = packed
    zero = jnp.zeros(sums.shape[2:], jnp.float32)
    sums[0, kept] = zero
    sums[1, kept] = zero

    pl.semaphore_wait(barrier, n + groups - 1)

    def meta_copy(off):
        return pltpu.make_async_remote_copy(
            src_ref=meta.at[z], dst_ref=meta.at[z],
            send_sem=meta_ss.at[off], recv_sem=meta_rs.at[z],
            device_id={"fsdp": lax.rem(z + off, n)}, device_id_type=MESH)

    def meta_arrived(p):
        return pltpu.make_async_remote_copy(
            src_ref=meta.at[p], dst_ref=meta.at[p],
            send_sem=meta_ss.at[0], recv_sem=meta_rs.at[p],
            device_id={"fsdp": p}, device_id_type=MESH)

    for off in range(1, n):
        meta_copy(off).start()
    local[0].wait()
    local[1].wait()

    def line(c, sub, up):
        to = jnp.minimum(z + 1, n - 1) if up else jnp.maximum(z - 1, 0)
        part = w.at[core, c, pl.ds(sub * half, half)]
        return pltpu.make_async_remote_copy(
            src_ref=part, dst_ref=part,
            send_sem=ag_ss.at[0 if up else 1, c, sub], recv_sem=ag_rs.at[c, sub],
            device_id={"fsdp": to}, device_id_type=MESH)

    def share(c, sub, which):
        part = w.at[which, c, pl.ds(sub * half, half)]
        return pltpu.make_async_remote_copy(
            src_ref=part, dst_ref=part,
            send_sem=sis_ss.at[c, sub], recv_sem=sis_rs.at[c, sub],
            device_id={"island": sister}, device_id_type=MESH)

    for sub in range(2):
        @pl.when(z < n - 1)
        def _():
            line(z, sub, True).start()

        @pl.when(z > 0)
        def _():
            line(z, sub, False).start()

    for b in range(row_blocks):
        pltpu.make_async_copy(
            tok_hbm.at[:, pl.ds(b * side, side)], tok.at[b], in_sem.at[2]).start()
    for b in range(row_blocks):
        pltpu.make_async_copy(
            cot_hbm.at[:, pl.ds(b * side, side)], cot.at[b], in_sem.at[3]).start()

    lane_i = lax.broadcasted_iota(jnp.int32, plan.shape, 1)
    row_j = lax.broadcasted_iota(jnp.int32, plan.shape, 0)
    wanted = jnp.full(plan.shape, -1, jnp.int32)
    for j in range(kept):
        wanted = jnp.where(lane_i == j, lax.div(down_at[0, j], row_blocks), wanted)
    wants[...] = wanted

    def forward(i):
        c = arrival(i, z, n)
        for sub in range(2):
            line(c, sub, True).wait_recv()

            @pl.when((c < z) & (z < n - 1))
            def _():
                line(c, sub, True).start()

            @pl.when((c > z) & (z > 0))
            def _():
                line(c, sub, False).start()

            share(c, sub, core).start()

    def tables():
        for off in range(1, n):
            meta_arrived(lax.rem(z + off, n)).wait_recv()
        wanted = wants[...]
        packed = jnp.zeros(plan.shape, jnp.int32)
        for m in range(2):
            mine = jnp.full(plan.shape, -1, jnp.int32)
            block = jnp.zeros(plan.shape, jnp.int32)
            there = []
            for i in range(n):
                got = meta[arrival(i, z, n)]
                for t in range(each):
                    q = m * each + t
                    c = jnp.broadcast_to(got[q:q + 1], plan.shape)
                    r = jnp.broadcast_to(got[2 * each + q:2 * each + q + 1], plan.shape)
                    here = lane_i == len(there)
                    mine = jnp.where(here, c, mine)
                    block = jnp.where(here, r, block)
                    there.append(c)
            before = jnp.full(plan.shape, kept, jnp.int32)
            found = before
            for k in range(kept):
                before = jnp.where((there[k] == mine) & (lane_i > k), k, before)
                found = jnp.where(there[k] == wanted, k, found)
            for at, value in ((m, before), (2 + m, found), (4 + m, block)):
                packed = jnp.where(row_j == at, value, packed)
        plan[...] = packed
        copy = pltpu.make_async_copy(plan, plan_s, meta_ls)
        copy.start()
        copy.wait()

    def project(i):
        c = arrival(i, z, n)
        for m in range(2):
            for t in range(each):
                prod[m, t] = jnp.dot(
                    tok[plan_s[4 + m, i * each + t]], w[m, c, t], preferred_element_type=jnp.float32)
        for t in range(each):
            slot = i * each + t
            for m in range(2):
                sums[m, slot] = sums[m, plan_s[m, slot]] + prod[m, t]

    def shared(i):
        c = arrival(i, z, n)
        for sub in range(2):
            share(c, sub, 1 - core).wait_recv()

    def start():
        tables()
        local[2].wait()
        project(0)

    middle = (z > 0) & (z < n - 1)
    if n == 4:
        @pl.when(middle)
        def _():
            for i in range(1, n):
                forward(i)
            start()
            for i in range(1, n):
                shared(i)
                project(i)

        @pl.when(jnp.logical_not(middle))
        def _():
            start()
            for i in range(1, n):
                forward(i)
                if 1 < i < n - 1:
                    shared(i - 1)
                    project(i - 1)
                if 1 < i == n - 2:
                    shared(i)
                    project(i)
            shared(n - 1)
            project(n - 1)
    else:
        forward(1)
        start()

        def gather(i, carry):
            @pl.when(i + 1 < n)
            def _():
                forward(i + 1)

            shared(i)
            project(i)
            return carry

        lax.fori_loop(1, n, gather, 0)
    local[3].wait()

    def pair(d, u):
        return pltpu.make_async_remote_copy(
            src_ref=give.at[d, u], dst_ref=take.at[d, u],
            send_sem=give_ss.at[d, u], recv_sem=give_rs.at[d, u],
            device_id={"island": sister}, device_id_type=MESH)

    def grad(j):
        g = sums[0, plan_s[2, j]]
        u = sums[1, plan_s[3, j]]
        e = jnp.exp(-jnp.abs(g))
        hidden = (g * jnp.where(g >= 0, 1.0, e) / (1.0 + e) * u).astype(jnp.bfloat16)
        return lax.dot_general(
            hidden, cot[lax.rem(down_at[0, j], row_blocks)], (((0,), (0,)), ((), ())),
            preferred_element_type=jnp.float32)

    def make(s):
        d = departure(s, z, n)
        for u in range(half):
            give[d, u] = grad(d * each + (1 - core) * half + u)
        for u in range(half):
            pair(d, u).start()
        for u in range(half):
            own[d, u] = grad(d * each + core * half + u)

    def hop(d, u):
        up = jnp.where(d > z, 0, 1)
        to = jnp.where(d > z, jnp.minimum(z + 1, n - 1), jnp.maximum(z - 1, 0))
        return pltpu.make_async_remote_copy(
            src_ref=own.at[d, u], dst_ref=moved.at[up, d, u],
            send_sem=rs_ss.at[d, u], recv_sem=rs_rs.at[up, d, u],
            device_id={"fsdp": to}, device_id_type=MESH)

    def came(up, d, u):
        return pltpu.make_async_remote_copy(
            src_ref=own.at[d, u], dst_ref=moved.at[up, d, u],
            send_sem=rs_ss.at[d, u], recv_sem=rs_rs.at[up, d, u],
            device_id={"fsdp": z}, device_id_type=MESH)

    def pass_on(s, u):
        d = departure(s, z, n)
        up = jnp.where(d > z, 0, 1)
        pair(d, u).wait_recv()

        @pl.when(middle)
        def _():
            came(up, d, u).wait_recv()
            own[d, u] = own[d, u] + take[d, u] + moved[up, d, u]

        @pl.when(jnp.logical_not(middle))
        def _():
            own[d, u] = own[d, u] + take[d, u]

        hop(d, u).start()

    def scatter(s):
        make(s + 1)
        for u in range(half):
            pass_on(s, u)

    if n == 4:
        @pl.when(middle)
        def _():
            for s in range(n):
                make(s)
            for s, u in sorted(
                ((s, u) for s in range(n - 1) for u in range(half)),
                key=lambda p: (min(p[0], 1) + p[1] if p[0] else 0, p[0]),
            ):
                pass_on(s, u)

        @pl.when(jnp.logical_not(middle))
        def _():
            for s in range(n):
                make(s)
                if s < n - 1:
                    for u in range(half):
                        pass_on(s, u)
    else:
        make(0)
        steps(n - 1, scatter)

    def last_hop(u):
        part = final.at[core * half + u]
        return pltpu.make_async_remote_copy(
            src_ref=part, dst_ref=part, send_sem=fin_ss.at[u], recv_sem=fin_rs.at[u],
            device_id={"island": sister}, device_id_type=MESH)

    def other_hop(u):
        part = final.at[(1 - core) * half + u]
        return pltpu.make_async_remote_copy(
            src_ref=part, dst_ref=part, send_sem=fin_ss.at[u], recv_sem=fin_rs.at[u],
            device_id={"island": sister}, device_id_type=MESH)

    def cross_hop(off, u):
        peer = lax.rem(group + off, groups) * 2 + core
        return pltpu.make_async_remote_copy(
            src_ref=cross.at[group, u], dst_ref=cross.at[group, u],
            send_sem=x_ss.at[off, u], recv_sem=x_rs.at[group, u],
            device_id={"island": peer}, device_id_type=MESH)

    def cross_came(off, u):
        there = lax.rem(group + off, groups)
        return pltpu.make_async_remote_copy(
            src_ref=cross.at[there, u], dst_ref=cross.at[there, u],
            send_sem=x_ss.at[off, u], recv_sem=x_rs.at[there, u],
            device_id={"island": there * 2 + core}, device_id_type=MESH)

    for u in range(half):
        pair(z, u).wait_recv()
        own[z, u] = own[z, u] + take[z, u]

        @pl.when(z > 0)
        def _():
            came(0, z, u).wait_recv()
            own[z, u] = own[z, u] + moved[0, z, u]

        @pl.when(z < n - 1)
        def _():
            came(1, z, u).wait_recv()
            own[z, u] = own[z, u] + moved[1, z, u]

        if groups > 1:
            cross[group, u] = own[z, u]
            for off in range(1, groups):
                cross_hop(off, u).start()
            for off in range(1, groups):
                cross_came(off, u).wait_recv()
            total = cross[0, u]
            for g in range(1, groups):
                total = total + cross[g, u]
            final[core * half + u] = total
        else:
            final[core * half + u] = own[z, u]
        last_hop(u).start()

    for u in range(half):
        other_hop(u).wait_recv()
    out_ref[...] = final[...]

    for u in range(half):
        last_hop(u).wait_send()
        for off in range(1, groups):
            cross_hop(off, u).wait_send()
    for off in range(1, n):
        meta_copy(off).wait_send()

    def drain(c):
        for sub in range(2):
            @pl.when((c <= z) & (z < n - 1))
            def _():
                line(c, sub, True).wait_send()

            @pl.when((c >= z) & (z > 0))
            def _():
                line(c, sub, False).wait_send()

            @pl.when(c != z)
            def _():
                share(c, sub, core).wait_send()
        for u in range(half):
            pair(c, u).wait_send()

            @pl.when(c != z)
            def _():
                hop(c, u).wait_send()

    steps(n, drain)


def body(
    tokens,
    cotangent,
    gate_tiles,
    up_tiles,
    gate_where,
    up_where,
    down_where,
    down_global,
    down_moment,
):
    n = lax.axis_size("fsdp")
    islands = lax.axis_size("island")
    groups = islands // 2
    each, _, side, _ = gate_tiles.shape
    half = each // 2
    kept = n * each
    count, width = tokens.shape
    col_blocks = FF // side // lax.axis_size("tensor")
    f32, bf16, i32 = jnp.float32, jnp.bfloat16, jnp.int32
    dma = pltpu.SemaphoreType.DMA
    smem = pl.BlockSpec(memory_space=pltpu.SMEM)
    anyw = pl.BlockSpec(memory_space=pl.ANY)
    summed = pl.pallas_call(
        functools.partial(kernel, n, groups, col_blocks),
        out_shape=jax.ShapeDtypeStruct((each, side, side), f32),
        in_specs=[smem] * 3 + [anyw] * 4,
        out_specs=pl.BlockSpec(memory_space=pltpu.VMEM),
        scratch_shapes=[
            pltpu.VMEM((width // side, count, side), bf16),
            pltpu.VMEM((width // side, count, side), bf16),
            pltpu.VMEM((2, n, each, side, side), bf16),
            pltpu.VMEM((n, 4 * each, side), i32),
            pltpu.VMEM((2, kept + 1, count, side), f32),
            pltpu.VMEM((2, each, count, side), f32),
            pltpu.VMEM((n, half, side, side), f32),
            pltpu.VMEM((n, half, side, side), f32),
            pltpu.VMEM((n, half, side, side), f32),
            pltpu.VMEM((2, n, half, side, side), f32),
            pltpu.VMEM((each, side, side), f32),
            pltpu.VMEM((groups, half, side, side), f32),
            pltpu.VMEM((8, side), i32),
            pltpu.VMEM((8, side), i32),
            pltpu.SMEM((8, side), i32),
            dma((4,)),
            dma((n,)),
            dma((n,)),
            dma,
            dma((2, n, 2)),
            dma((n, 2)),
            dma((n, 2)),
            dma((n, 2)),
            dma((n, half)),
            dma((n, half)),
            dma((n, half)),
            dma((2, n, half)),
            dma((half,)),
            dma((half,)),
            dma((groups, half)),
            dma((groups, half)),
        ],
        compiler_params=pltpu.CompilerParams(
            collective_id=0, has_side_effects=True, vmem_limit_bytes=60 * 1024 * 1024
        ),
        cost_estimate=pl.CostEstimate(
            flops=6 * kept * count * side * side,
            bytes_accessed=2 * tokens.size * 2,
            transcendentals=kept * count * side,
        ),
    )(gate_where.T, up_where.T, down_where.T, gate_tiles[:, 0], up_tiles[:, 0], tokens, cotangent)
    master = down_global[:, 0]
    moment = down_moment[:, 0]
    average = inner_rate * (summed / islands + decay_rate * master)
    fresh_moment = momentum_rate * moment + average
    fresh_master = master - outer_rate * (average + momentum_rate * fresh_moment)
    return (fresh_master[:, None], fresh_moment[:, None])


def solution(mesh):
    placed = (
        P(("island", "fsdp"), None),
        P(("island", "fsdp"), None),
        P("fsdp", "tensor", None, None),
        P("fsdp", "tensor", None, None),
        P("fsdp", "tensor"),
        P("fsdp", "tensor"),
        P(None, "tensor"),
        P("fsdp", "tensor", None, None),
        P("fsdp", "tensor", None, None),
    )
    return jax.shard_map(
        body,
        mesh=mesh,
        in_specs=placed,
        out_specs=(P("fsdp", "tensor", None, None), P("fsdp", "tensor", None, None)),
        check_vma=False,
    )
```

```python
import functools

import jax
import jax.numpy as jnp
from jax import lax
from jax.experimental import pallas as pl
from jax.experimental.pallas import tpu as pltpu
from jax.sharding import PartitionSpec as P

FF = 36864
MESH = pl.DeviceIdType.MESH

inner_rate = 0.5
decay_rate = 0.1
outer_rate = 0.7
momentum_rate = 0.9


def steps(count, step):
    if count <= 4:
        for i in range(count):
            step(i)
    else:
        lax.fori_loop(0, count, lambda i, c: (step(i), c)[1], 0)


def arrival(i, z, n):
    close = jnp.minimum(z, n - 1 - z)
    near = jnp.where(i % 2 == 1, z - (i + 1) // 2, z + i // 2)
    far = jnp.where(z < n - 1 - z, i, n - 1 - i)
    return jnp.where(i <= 2 * close, near, far)


def departure(s, z, n):
    close = jnp.minimum(z, n - 1 - z)
    own = 2 * close + 1
    at = s + jnp.where(s >= own, 1, 0)
    side = jnp.where(at % 2 == 0, n - 1 - at // 2, (at - 1) // 2)
    side = jnp.where(z < n - 1 - z, side, n - 1 - side)
    return jnp.where(s == n - 1, z, side)


def kernel(
    n, groups, col_blocks,
    gate_at, up_at, down_at, gate_hbm, up_hbm, tok_hbm, cot_hbm,
    out_ref,
    tok, cot, w, meta, sums, prod, own, give, take, moved, final, cross,
    meta_s, cols, rows, prev, last,
    in_sem, meta_ss, meta_rs, meta_ls, ag_ss, ag_rs, sis_ss, sis_rs,
    give_ss, give_rs, rs_ss, rs_rs, fin_ss, fin_rs, x_ss, x_rs,
):
    z = lax.axis_index("fsdp")
    isl = lax.axis_index("island")
    core = lax.rem(isl, 2)
    group = lax.div(isl, 2)
    sister = isl + 1 - 2 * core
    each = gate_hbm.shape[0]
    half = each // 2
    kept = n * each
    side = gate_hbm.shape[-1]
    row_blocks = tok_hbm.shape[1] // side

    local = [
        pltpu.make_async_copy(gate_hbm, w.at[0, z], in_sem.at[0]),
        pltpu.make_async_copy(up_hbm, w.at[1, z], in_sem.at[1]),
        pltpu.make_async_copy(tok, tok, in_sem.at[2]),
        pltpu.make_async_copy(cot, cot, in_sem.at[3]),
    ]
    local[0].start()
    local[1].start()

    barrier = pltpu.get_barrier_semaphore()
    for off in range(1, n):
        pl.semaphore_signal(barrier, inc=1, device_id={"fsdp": lax.rem(z + off, n)}, device_id_type=MESH)
    pl.semaphore_signal(barrier, inc=1, device_id={"island": sister}, device_id_type=MESH)
    for off in range(1, groups):
        peer = lax.rem(group + off, groups) * 2 + core
        pl.semaphore_signal(barrier, inc=1, device_id={"island": peer}, device_id_type=MESH)

    row_i = lax.broadcasted_iota(jnp.int32, (2 * each, side), 0)
    lane_i = lax.broadcasted_iota(jnp.int32, (2 * each, side), 1)
    packed = jnp.zeros((2 * each, side), jnp.int32)
    for q in range(2 * each):
        cell = gate_at[0, q] if q < each else up_at[0, q - each]
        r = lax.div(cell, col_blocks)
        c = cell - r * col_blocks
        packed = jnp.where(row_i == q, jnp.where(lane_i == 0, r, c), packed)
    meta[z] = packed
    zero = jnp.zeros(sums.shape[2:], jnp.float32)
    sums[0, kept] = zero
    sums[1, kept] = zero

    pl.semaphore_wait(barrier, n + groups - 1)

    def meta_copy(off):
        return pltpu.make_async_remote_copy(
            src_ref=meta.at[z], dst_ref=meta.at[z],
            send_sem=meta_ss.at[off], recv_sem=meta_rs.at[z],
            device_id={"fsdp": lax.rem(z + off, n)}, device_id_type=MESH)

    def meta_arrived(p):
        return pltpu.make_async_remote_copy(
            src_ref=meta.at[p], dst_ref=meta.at[p],
            send_sem=meta_ss.at[0], recv_sem=meta_rs.at[p],
            device_id={"fsdp": p}, device_id_type=MESH)

    for off in range(1, n):
        meta_copy(off).start()
    local[0].wait()
    local[1].wait()

    def line(c, sub, up):
        to = jnp.minimum(z + 1, n - 1) if up else jnp.maximum(z - 1, 0)
        part = w.at[core, c, pl.ds(sub, 1)]
        return pltpu.make_async_remote_copy(
            src_ref=part, dst_ref=part,
            send_sem=ag_ss.at[0 if up else 1, c, sub], recv_sem=ag_rs.at[c, sub],
            device_id={"fsdp": to}, device_id_type=MESH)

    def share(c, sub, which):
        part = w.at[which, c, pl.ds(sub, 1)]
        return pltpu.make_async_remote_copy(
            src_ref=part, dst_ref=part,
            send_sem=sis_ss.at[c, sub], recv_sem=sis_rs.at[c, sub],
            device_id={"island": sister}, device_id_type=MESH)

    for sub in range(each):
        @pl.when(z < n - 1)
        def _():
            line(z, sub, True).start()

        @pl.when(z > 0)
        def _():
            line(z, sub, False).start()

    for b in range(row_blocks):
        pltpu.make_async_copy(
            tok_hbm.at[:, pl.ds(b * side, side)], tok.at[b], in_sem.at[2]).start()
    for b in range(row_blocks):
        pltpu.make_async_copy(
            cot_hbm.at[:, pl.ds(b * side, side)], cot.at[b], in_sem.at[3]).start()

    def forward(i):
        c = arrival(i, z, n)
        for sub in range(each):
            line(c, sub, True).wait_recv()

            @pl.when((c < z) & (z < n - 1))
            def _():
                line(c, sub, True).start()

            @pl.when((c > z) & (z > 0))
            def _():
                line(c, sub, False).start()

            share(c, sub, core).start()

    def tables():
        for off in range(1, n):
            meta_arrived(lax.rem(z + off, n)).wait_recv()
        copy = pltpu.make_async_copy(meta, meta_s, meta_ls)
        copy.start()
        copy.wait()
        for m in range(2):
            def read(i):
                c = arrival(i, z, n)
                for t in range(each):
                    rows[m, i * each + t] = meta_s[c, m * each + t, 0]
                    cols[m, i * each + t] = meta_s[c, m * each + t, 1]

            steps(n, read)

            def link(i, carry):
                mine = cols[m, i]
                wanted = lax.div(down_at[0, i], row_blocks)
                before = jnp.int32(kept)
                found = jnp.int32(kept)
                for k in range(kept):
                    there = cols[m, k]
                    before = jnp.where((there == mine) & (k < i), k, before)
                    found = jnp.where(there == wanted, k, found)
                prev[m, i] = before
                last[m, i] = found
                return carry

            lax.fori_loop(0, kept, link, 0)

    def project(i):
        c = arrival(i, z, n)
        for m in range(2):
            for t in range(each):
                prod[m, t] = jnp.dot(
                    tok[rows[m, i * each + t]], w[m, c, t], preferred_element_type=jnp.float32)
        for t in range(each):
            slot = i * each + t
            for m in range(2):
                sums[m, slot] = sums[m, prev[m, slot]] + prod[m, t]

    def shared(i):
        c = arrival(i, z, n)
        for sub in range(each):
            share(c, sub, 1 - core).wait_recv()

    def start():
        tables()
        local[2].wait()
        project(0)

    middle = (z > 0) & (z < n - 1)
    if n == 4:
        @pl.when(middle)
        def _():
            for i in range(1, n - 1):
                forward(i)
            tables()
            local[2].wait()
            forward(n - 1)
            project(0)
            for i in range(1, n):
                shared(i)
                project(i)

        @pl.when(jnp.logical_not(middle))
        def _():
            start()
            for i in range(1, n):
                forward(i)
                if 1 < i < n - 1:
                    shared(i - 1)
                    project(i - 1)
                if 1 < i == n - 2:
                    shared(i)
                    project(i)
            shared(n - 1)
            project(n - 1)
    else:
        forward(1)
        start()

        def gather(i, carry):
            @pl.when(i + 1 < n)
            def _():
                forward(i + 1)

            shared(i)
            project(i)
            return carry

        lax.fori_loop(1, n, gather, 0)
    local[3].wait()

    def pair(d, u):
        return pltpu.make_async_remote_copy(
            src_ref=give.at[d, u], dst_ref=take.at[d, u],
            send_sem=give_ss.at[d, u], recv_sem=give_rs.at[d, u],
            device_id={"island": sister}, device_id_type=MESH)

    def grad(j):
        g = sums[0, last[0, j]]
        u = sums[1, last[1, j]]
        e = jnp.exp(-jnp.abs(g))
        hidden = (g * jnp.where(g >= 0, 1.0, e) / (1.0 + e) * u).astype(jnp.bfloat16)
        return lax.dot_general(
            hidden, cot[lax.rem(down_at[0, j], row_blocks)], (((0,), (0,)), ((), ())),
            preferred_element_type=jnp.float32)

    def make(s):
        d = departure(s, z, n)
        for u in range(half):
            give[d, u] = grad(d * each + (1 - core) * half + u)
        for u in range(half):
            pair(d, u).start()
        for u in range(half):
            own[d, u] = grad(d * each + core * half + u)

    def hop(d, u):
        up = jnp.where(d > z, 0, 1)
        to = jnp.where(d > z, jnp.minimum(z + 1, n - 1), jnp.maximum(z - 1, 0))
        return pltpu.make_async_remote_copy(
            src_ref=own.at[d, u], dst_ref=moved.at[up, d, u],
            send_sem=rs_ss.at[d, u], recv_sem=rs_rs.at[up, d, u],
            device_id={"fsdp": to}, device_id_type=MESH)

    def came(up, d, u):
        return pltpu.make_async_remote_copy(
            src_ref=own.at[d, u], dst_ref=moved.at[up, d, u],
            send_sem=rs_ss.at[d, u], recv_sem=rs_rs.at[up, d, u],
            device_id={"fsdp": z}, device_id_type=MESH)

    def pass_on(s):
        d = departure(s, z, n)
        up = jnp.where(d > z, 0, 1)
        for u in range(half):
            pair(d, u).wait_recv()

            @pl.when(middle)
            def _():
                came(up, d, u).wait_recv()
                own[d, u] = own[d, u] + take[d, u] + moved[up, d, u]

            @pl.when(jnp.logical_not(middle))
            def _():
                own[d, u] = own[d, u] + take[d, u]

            hop(d, u).start()

    def scatter(s):
        make(s + 1)
        pass_on(s)

    if n == 4:
        @pl.when(middle)
        def _():
            for s in range(n):
                make(s)
            for s in range(n - 1):
                pass_on(s)

        @pl.when(jnp.logical_not(middle))
        def _():
            make(0)
            for s in range(n - 1):
                scatter(s)
    else:
        make(0)
        steps(n - 1, scatter)

    def last_hop(u):
        part = final.at[core * half + u]
        return pltpu.make_async_remote_copy(
            src_ref=part, dst_ref=part, send_sem=fin_ss.at[u], recv_sem=fin_rs.at[u],
            device_id={"island": sister}, device_id_type=MESH)

    def other_hop(u):
        part = final.at[(1 - core) * half + u]
        return pltpu.make_async_remote_copy(
            src_ref=part, dst_ref=part, send_sem=fin_ss.at[u], recv_sem=fin_rs.at[u],
            device_id={"island": sister}, device_id_type=MESH)

    def cross_hop(off, u):
        peer = lax.rem(group + off, groups) * 2 + core
        return pltpu.make_async_remote_copy(
            src_ref=cross.at[group, u], dst_ref=cross.at[group, u],
            send_sem=x_ss.at[off, u], recv_sem=x_rs.at[group, u],
            device_id={"island": peer}, device_id_type=MESH)

    def cross_came(off, u):
        there = lax.rem(group + off, groups)
        return pltpu.make_async_remote_copy(
            src_ref=cross.at[there, u], dst_ref=cross.at[there, u],
            send_sem=x_ss.at[off, u], recv_sem=x_rs.at[there, u],
            device_id={"island": there * 2 + core}, device_id_type=MESH)

    for u in range(half):
        pair(z, u).wait_recv()
        own[z, u] = own[z, u] + take[z, u]

        @pl.when(z > 0)
        def _():
            came(0, z, u).wait_recv()
            own[z, u] = own[z, u] + moved[0, z, u]

        @pl.when(z < n - 1)
        def _():
            came(1, z, u).wait_recv()
            own[z, u] = own[z, u] + moved[1, z, u]

        if groups > 1:
            cross[group, u] = own[z, u]
            for off in range(1, groups):
                cross_hop(off, u).start()
            for off in range(1, groups):
                cross_came(off, u).wait_recv()
            total = cross[0, u]
            for g in range(1, groups):
                total = total + cross[g, u]
            final[core * half + u] = total
        else:
            final[core * half + u] = own[z, u]
        last_hop(u).start()

    for u in range(half):
        other_hop(u).wait_recv()
    out_ref[...] = final[...]

    for u in range(half):
        last_hop(u).wait_send()
        for off in range(1, groups):
            cross_hop(off, u).wait_send()
    for off in range(1, n):
        meta_copy(off).wait_send()

    def drain(c):
        for sub in range(each):
            @pl.when((c <= z) & (z < n - 1))
            def _():
                line(c, sub, True).wait_send()

            @pl.when((c >= z) & (z > 0))
            def _():
                line(c, sub, False).wait_send()

            @pl.when(c != z)
            def _():
                share(c, sub, core).wait_send()
        for u in range(half):
            pair(c, u).wait_send()

            @pl.when(c != z)
            def _():
                hop(c, u).wait_send()

    steps(n, drain)


def body(
    tokens,
    cotangent,
    gate_tiles,
    up_tiles,
    gate_where,
    up_where,
    down_where,
    down_global,
    down_moment,
):
    n = lax.axis_size("fsdp")
    islands = lax.axis_size("island")
    groups = islands // 2
    each, _, side, _ = gate_tiles.shape
    half = each // 2
    kept = n * each
    count, width = tokens.shape
    col_blocks = FF // side // lax.axis_size("tensor")
    f32, bf16, i32 = jnp.float32, jnp.bfloat16, jnp.int32
    dma = pltpu.SemaphoreType.DMA
    smem = pl.BlockSpec(memory_space=pltpu.SMEM)
    anyw = pl.BlockSpec(memory_space=pl.ANY)
    summed = pl.pallas_call(
        functools.partial(kernel, n, groups, col_blocks),
        out_shape=jax.ShapeDtypeStruct((each, side, side), f32),
        in_specs=[smem] * 3 + [anyw] * 4,
        out_specs=pl.BlockSpec(memory_space=pltpu.VMEM),
        scratch_shapes=[
            pltpu.VMEM((width // side, count, side), bf16),
            pltpu.VMEM((width // side, count, side), bf16),
            pltpu.VMEM((2, n, each, side, side), bf16),
            pltpu.VMEM((n, 2 * each, side), i32),
            pltpu.VMEM((2, kept + 1, count, side), f32),
            pltpu.VMEM((2, each, count, side), f32),
            pltpu.VMEM((n, half, side, side), f32),
            pltpu.VMEM((n, half, side, side), f32),
            pltpu.VMEM((n, half, side, side), f32),
            pltpu.VMEM((2, n, half, side, side), f32),
            pltpu.VMEM((each, side, side), f32),
            pltpu.VMEM((groups, half, side, side), f32),
            pltpu.SMEM((n, 2 * each, side), i32),
            pltpu.SMEM((2, kept), i32),
            pltpu.SMEM((2, kept), i32),
            pltpu.SMEM((2, kept), i32),
            pltpu.SMEM((2, kept), i32),
            dma((4,)),
            dma((n,)),
            dma((n,)),
            dma,
            dma((2, n, each)),
            dma((n, each)),
            dma((n, each)),
            dma((n, each)),
            dma((n, half)),
            dma((n, half)),
            dma((n, half)),
            dma((2, n, half)),
            dma((half,)),
            dma((half,)),
            dma((groups, half)),
            dma((groups, half)),
        ],
        compiler_params=pltpu.CompilerParams(
            collective_id=0, has_side_effects=True, vmem_limit_bytes=60 * 1024 * 1024
        ),
        cost_estimate=pl.CostEstimate(
            flops=6 * kept * count * side * side,
            bytes_accessed=2 * tokens.size * 2,
            transcendentals=kept * count * side,
        ),
    )(gate_where.T, up_where.T, down_where.T, gate_tiles[:, 0], up_tiles[:, 0], tokens, cotangent)
    master = down_global[:, 0]
    moment = down_moment[:, 0]
    average = inner_rate * (summed / islands + decay_rate * master)
    fresh_moment = momentum_rate * moment + average
    fresh_master = master - outer_rate * (average + momentum_rate * fresh_moment)
    return (fresh_master[:, None], fresh_moment[:, None])


def solution(mesh):
    placed = (
        P(("island", "fsdp"), None),
        P(("island", "fsdp"), None),
        P("fsdp", "tensor", None, None),
        P("fsdp", "tensor", None, None),
        P("fsdp", "tensor"),
        P("fsdp", "tensor"),
        P(None, "tensor"),
        P("fsdp", "tensor", None, None),
        P("fsdp", "tensor", None, None),
    )
    return jax.shard_map(
        body,
        mesh=mesh,
        in_specs=placed,
        out_specs=(P("fsdp", "tensor", None, None), P("fsdp", "tensor", None, None)),
        check_vma=False,
    )
```
